512 devices in a mesh: tap: 64 (over y_hi, x, z), tm: 8 (over y_lo, core).
Axes of the slice: x: 4, y: 8 (y_hi: 2, y_lo: 4; y = y_hi * 4 + y_lo), z: 8, core: 2. Of those that a mesh axis runs over, the one named last changes fastest.
Arguments:
- pressure: bfloat16 [2048, 8192], P('tap', 'tm'), may hold values from -12 to 12
- filters: float32 [2, 16], replicated, may hold values from -1.5 to 1.5
Outputs:
- scalograms: float32 [3, 2048, 2048], P(None, 'tap', 'tm')
The draws below stay inside these ranges and needn't reach their ends.
All inputs are finite; a program needn't handle non-finite values.
Results may differ from the reference program's by a relative error of at most 0.0003.
Values may be sent and summed in bfloat16 or wider, within the bound.
A program may use at most 128 MiB of HBM per device.

```python
import jax
import jax.numpy as jnp

TAPS = 2048
FILT = 16
LEVELS = 3
SAMPLES = 8192


def draw_pressure(key, part):
    subkeys = jax.random.split(key, 7)
    sources = jax.random.truncated_normal(subkeys[0], -4.0, 4.0, (8, SAMPLES), jnp.float32)
    own_noise = jax.random.truncated_normal(subkeys[1], -4.0, 4.0, (TAPS, SAMPLES), jnp.float32)
    first_source = jax.random.randint(subkeys[2], (TAPS,), 0, 8)
    second_source = (first_source + jax.random.randint(subkeys[3], (TAPS,), 1, 8)) % 8
    weight_one = jax.random.uniform(subkeys[4], (TAPS, 1), jnp.float32, 0.3, 1.0)
    weight_two = jax.random.uniform(subkeys[5], (TAPS, 1), jnp.float32, 0.3, 1.0)
    weight_own = jax.random.uniform(subkeys[6], (TAPS, 1), jnp.float32, 0.3, 1.0)
    mixture = weight_one * sources[first_source] + weight_two * sources[second_source] + weight_own * own_noise
    return mixture.astype(jnp.bfloat16)


def bell_draw(own_key, extent, width, most, kind=jnp.bfloat16):
    drawn = width * jax.random.normal(own_key, extent, jnp.float32)
    return jnp.clip(drawn, min=-most, max=most).astype(kind)


def setup_inputs(seed: int = 0) -> dict:
    seeds = jax.random.split(jax.random.key(seed), 3)
    return {
        "pressure": draw_pressure(jax.random.fold_in(seeds[2], 71), 0),
        "filters": bell_draw(seeds[1], (2, FILT), FILT ** -0.5, 1.5, jnp.float32),
    }


def reference(pressure, filters):
    series = pressure.astype(jnp.float32)
    centre = FILT // 2
    scalogram_list = []
    for level_index in range(LEVELS):
        dilation = 2 ** level_index
        detail = jnp.zeros(series.shape, jnp.float32)
        smooth = jnp.zeros(series.shape, jnp.float32)
        for offset in range(FILT):
            shifted = jnp.roll(series, -(offset - centre) * dilation, axis=1)
            detail = detail + filters[0, offset] * shifted
            smooth = smooth + filters[1, offset] * shifted
        coeffs = detail.astype(jnp.bfloat16)
        cross_tile = jnp.dot(coeffs, coeffs.T, preferred_element_type=jnp.float32) * (1.0 / SAMPLES)
        scalogram_list.append(cross_tile)
        series = smooth
    return jnp.stack(scalogram_list)
```

```python
import jax
import jax.numpy as jnp
from jax import lax
from jax.experimental import pallas as pl
from jax.experimental.pallas import tpu as pltpu
from jax.sharding import PartitionSpec as P

FILT = 16
LEVELS = 3
NX, NZ, NYH, NYL = 4, 8, 2, 4
ROWS = 32
WIDTH = 1024
HALO = 128
EXT = WIDTH + HALO
WIN = 256
OUT = 128
NWIN = WIDTH // OUT
SPLITS = 3
LANES = 384
MESH = pl.DeviceIdType.MESH
NT = (((1,), (1,)), ((), ()))


def remote(src, dst, send, recv, tap, tm):
    return pltpu.make_async_remote_copy(
        src_ref=src, dst_ref=dst, send_sem=send, recv_sem=recv,
        device_id=(tap, tm), device_id_type=MESH,
    )


def build_bands(f_ref, wbuf):
    lane = lax.broadcasted_iota(jnp.int32, (8, LANES), 1)

    def comb(row, top, step):
        line = jnp.zeros((8, LANES), jnp.float32)
        for k in range(FILT):
            line = jnp.where(lane == top - step * k, f_ref[row, k], line)
        return line

    def smoothed(line, step):
        total = jnp.zeros((8, LANES), jnp.float32)
        for k in range(FILT):
            moved = line if k == 0 else pltpu.roll(line, LANES - step * k, 1)
            total = total + f_ref[1, k] * moved
        return total

    lines = [
        comb(0, 328, 1),
        smoothed(comb(0, 344, 2), 1),
        smoothed(smoothed(comb(0, 376, 4), 2), 1),
    ]
    for level, line in enumerate(lines):
        wide = jnp.broadcast_to(line[0:1, :], (WIN, LANES))
        band = pltpu.roll(wide, 0, 1, stride=1, stride_axis=0)[:, :OUT]
        for piece in range(SPLITS):
            part = band.astype(jnp.bfloat16)
            wbuf[piece, :, level * OUT : (level + 1) * OUT] = part
            band = band - part.astype(jnp.float32)


def details_of(rows_ext, wbuf):
    windows = jnp.concatenate(
        [rows_ext[:, w * OUT : w * OUT + WIN] for w in range(NWIN)], axis=0
    )
    total = jnp.dot(windows, wbuf[0], preferred_element_type=jnp.float32)
    for piece in range(1, SPLITS):
        total += jnp.dot(windows, wbuf[piece], preferred_element_type=jnp.float32)
    return total.astype(jnp.bfloat16)


def kernel(
    p_ref, f_ref, o_ref,
    pbuf, qbuf, wbuf, dp, dq, part, sib, red, xo, yo,
    hs, hr, xs, xr, cs, cr, zps, zpr, zms, zmr, ss, sr, xos, xor_, yos, yor,
):
    a = lax.axis_index("tap")
    b = lax.axis_index("tm")
    y_hi = a // (NX * NZ)
    x = (a // NZ) % NX
    z = a % NZ
    y_lo = b // 2
    core = b % 2

    def tap_of(yh, xx, zz):
        return yh * (NX * NZ) + xx * NZ + zz

    b_next = (b + 1) % 8
    b_prev = (b + 7) % 8
    home = y_hi == x // 2
    far_x = 2 * y_hi + x // 2
    far_tap = tap_of(1 - y_hi, far_x, z)
    z_up = tap_of(y_hi, x, (z + 1) % NZ)
    z_down = tap_of(y_hi, x, (z + NZ - 1) % NZ)
    sibling = y_lo * 2 + (1 - core)

    barrier = pltpu.get_barrier_semaphore()

    def hello(tap, tm):
        pl.semaphore_signal(barrier, inc=1, device_id=(tap, tm), device_id_type=MESH)

    hello(a, b_next)
    hello(a, b_prev)
    for d in range(1, 4):
        hello(a, (b + 2 * d) % 8)
        hello(tap_of(y_hi, (x + d) % NX, z), b)
    hello(z_up, b)
    hello(z_down, b)
    hello(far_tap, b)

    @pl.when(jnp.logical_not(home))
    def _():
        for s in range(2):
            hello(tap_of(1 - y_hi, 2 * (x % 2) + s, z), b)

    pbuf[x, :, 0:WIDTH] = p_ref[...]
    pl.semaphore_wait(barrier, jnp.where(home, 11, 13))

    halo = remote(
        p_ref.at[:, pl.ds(0, HALO)], pbuf.at[x, :, pl.ds(WIDTH, HALO)],
        hs.at[0], hr.at[0], a, b_prev,
    )
    halo.start()
    build_bands(f_ref, wbuf)
    halo.wait_recv()

    cross = remote(pbuf.at[x], qbuf.at[z, x % 2], cs.at[0], cr.at[x % 2], far_tap, b)
    cross.start()
    ring = []
    for d in range(1, 4):
        ring.append(remote(
            pbuf.at[x], pbuf.at[x], xs.at[d - 1], xr.at[d - 1],
            tap_of(y_hi, (x + d) % NX, z), b,
        ))
        ring[-1].start()
    for d in range(1, 4):
        slot = pbuf.at[(x + NX - d) % NX]
        remote(slot, slot, xs.at[d - 1], xr.at[d - 1], z_up, b).wait_recv()

    @pl.when(home)
    def _():
        for s in range(2):
            qbuf[z, s] = pbuf[2 * (x % 2) + s]

    @pl.when(jnp.logical_not(home))
    def _():
        for s in range(2):
            slot = qbuf.at[z, s]
            remote(slot, slot, cs.at[0], cr.at[s], far_tap, b).wait_recv()

    sends = [halo, cross] + ring

    def up(k, s):
        slot = qbuf.at[(z + NZ - k) % NZ, s]
        sends.append(remote(slot, slot, zps.at[2 * k + s], zpr.at[2 * k + s], z_up, b))
        sends[-1].start()

    def down(k, s):
        slot = qbuf.at[(z + k) % NZ, s]
        sends.append(remote(slot, slot, zms.at[2 * k + s], zmr.at[2 * k + s], z_down, b))
        sends[-1].start()

    def from_below(k, s):
        slot = qbuf.at[(z + 2 * NZ - 1 - k) % NZ, s]
        remote(slot, slot, zps.at[2 * k + s], zpr.at[2 * k + s], z_up, b).wait_recv()

    def from_above(k, s):
        slot = qbuf.at[(z + 1 + k) % NZ, s]
        remote(slot, slot, zms.at[2 * k + s], zmr.at[2 * k + s], z_down, b).wait_recv()

    def columns(m):
        zz = (z + m) % NZ
        ext = jnp.concatenate([qbuf[zz, 0], qbuf[zz, 1]], axis=0)
        val = details_of(ext, wbuf)
        for w in range(NWIN):
            for s in range(2):
                first = w * 2 * ROWS + s * ROWS
                for j in range(LEVELS):
                    dq[j, s * 256 + m * ROWS : s * 256 + (m + 1) * ROWS, w * OUT : (w + 1) * OUT] = (
                        val[first : first + ROWS, j * OUT : (j + 1) * OUT]
                    )

    for s in range(2):
        up(0, s)
        down(0, s)

    rows_ext = jnp.concatenate([pbuf[i] for i in range(NX)], axis=0)
    val = details_of(rows_ext, wbuf)
    for w in range(NWIN):
        for j in range(LEVELS):
            dp[j, :, w * OUT : (w + 1) * OUT] = val[
                w * NX * ROWS : (w + 1) * NX * ROWS, j * OUT : (j + 1) * OUT
            ]
    columns(0)
    for k in range(3):
        for s in range(2):
            from_below(k, s)
            if k < 2 or s == 0:
                up(k + 1, s)
            from_above(k, s)
            if k < 2 or s == 1:
                down(k + 1, s)
        columns(1 + k)
        columns(7 - k)
    from_below(3, 0)
    from_above(3, 1)
    columns(4)

    for j in range(LEVELS):
        prod = lax.dot_general(dp[j], dq[j], NT, preferred_element_type=jnp.float32)
        for s in range(2):
            part[s, j] = prod[:, s * 256 : (s + 1) * 256]

    pair = remote(part.at[1 - core], sib, ss.at[0], sr.at[0], a, sibling)
    pair.start()
    pair.wait_recv()
    sends.append(pair)
    for i in range(NX):
        for j in range(LEVELS):
            red[i, j] = part[core, j, i * ROWS : (i + 1) * ROWS] + sib[j, i * ROWS : (i + 1) * ROWS]

    for d in range(1, 4):
        there = (x + d) % NX
        sends.append(remote(
            red.at[there], xo.at[x], xos.at[d - 1], xor_.at[d - 1], tap_of(y_hi, there, z), b
        ))
        sends[-1].start()
    xo[x] = red[x]
    for d in range(1, 4):
        slot = xo.at[(x + NX - d) % NX]
        remote(slot, slot, xos.at[d - 1], xor_.at[d - 1], z_up, b).wait_recv()

    for d in range(1, 4):
        there = (y_lo + d) % NYL
        sends.append(remote(
            xo.at[there], yo.at[d - 1], yos.at[d - 1], yor.at[d - 1], a, there * 2 + core
        ))
        sends[-1].start()
    total = xo[y_lo]
    for d in range(1, 4):
        slot = yo.at[d - 1]
        remote(slot, slot, yos.at[d - 1], yor.at[d - 1], a, sibling).wait_recv()
    total = total + (yo[0] + yo[1] + yo[2])
    total = total * (1.0 / (WIDTH * 8))
    for j in range(LEVELS):
        o_ref[j] = pltpu.roll(total[j], z * ROWS, 1)
    for copy in sends:
        copy.wait_send()


def body(pressure, filters):
    dma = pltpu.SemaphoreType.DMA
    return pl.pallas_call(
        kernel,
        out_shape=jax.ShapeDtypeStruct((LEVELS, ROWS, 256), jnp.float32),
        in_specs=[
            pl.BlockSpec(memory_space=pltpu.VMEM),
            pl.BlockSpec(memory_space=pltpu.SMEM),
        ],
        out_specs=pl.BlockSpec(memory_space=pltpu.VMEM),
        scratch_shapes=[
            pltpu.VMEM((NX, ROWS, EXT), jnp.bfloat16),
            pltpu.VMEM((NZ, 2, ROWS, EXT), jnp.bfloat16),
            pltpu.VMEM((SPLITS, WIN, LEVELS * OUT), jnp.bfloat16),
            pltpu.VMEM((LEVELS, NX * ROWS, WIDTH), jnp.bfloat16),
            pltpu.VMEM((LEVELS, 512, WIDTH), jnp.bfloat16),
            pltpu.VMEM((2, LEVELS, NX * ROWS, 256), jnp.float32),
            pltpu.VMEM((LEVELS, NX * ROWS, 256), jnp.float32),
            pltpu.VMEM((NX, LEVELS, ROWS, 256), jnp.float32),
            pltpu.VMEM((NX, LEVELS, ROWS, 256), jnp.float32),
            pltpu.VMEM((3, LEVELS, ROWS, 256), jnp.float32),
            dma((1,)), dma((1,)),
            dma((3,)), dma((3,)),
            dma((1,)), dma((2,)),
            dma((8,)), dma((8,)),
            dma((8,)), dma((8,)),
            dma((1,)), dma((1,)),
            dma((3,)), dma((3,)),
            dma((3,)), dma((3,)),
        ],
        compiler_params=pltpu.CompilerParams(
            collective_id=0, has_side_effects=True, vmem_limit_bytes=40 * 1024 * 1024
        ),
        cost_estimate=pl.CostEstimate(
            flops=4_000_000_000, bytes_accessed=200_000, transcendentals=0
        ),
    )(pressure, filters)


def solution(mesh):
    placed = (P("tap", "tm"), P())
    return jax.shard_map(
        body, mesh=mesh, in_specs=placed, out_specs=P(None, "tap", "tm"), check_vma=False
    )
```

```python
import jax
import jax.numpy as jnp
from jax import lax
from jax.experimental import pallas as pl
from jax.experimental.pallas import tpu as pltpu
from jax.sharding import PartitionSpec as P

FILT = 16
LEVELS = 3
NX, NZ, NYL = 4, 8, 4
ROWS = 32
WIDTH = 1024
HALO = 128
WIN = 256
OUT = 128
NWIN = WIDTH // OUT
SPLITS = 3
LANES = 384
CHUNKS = 4
HALF = 16
PIECE = {1: (0, 0), 7: (0, 1), 2: (1, 0), 6: (1, 1), 3: (2, 0), 5: (2, 1), 0: (3, 0), 4: (3, 1)}
MESH = pl.DeviceIdType.MESH
NT = (((1,), (1,)), ((), ()))


def remote(src, dst, send, recv, tap, tm):
    return pltpu.make_async_remote_copy(
        src_ref=src, dst_ref=dst, send_sem=send, recv_sem=recv,
        device_id=(tap, tm), device_id_type=MESH,
    )


def build_bands(f_ref, wbuf):
    lane = lax.broadcasted_iota(jnp.int32, (8, LANES), 1)

    def comb(row, top, step):
        line = jnp.zeros((8, LANES), jnp.float32)
        for k in range(FILT):
            line = jnp.where(lane == top - step * k, f_ref[row, k], line)
        return line

    def smoothed(line, step):
        total = jnp.zeros((8, LANES), jnp.float32)
        for k in range(FILT):
            moved = line if k == 0 else pltpu.roll(line, LANES - step * k, 1)
            total = total + f_ref[1, k] * moved
        return total

    lines = [
        comb(0, 328, 1),
        smoothed(comb(0, 344, 2), 1),
        smoothed(smoothed(comb(0, 376, 4), 2), 1),
    ]
    for level, line in enumerate(lines):
        wide = jnp.broadcast_to(line[0:1, :], (WIN, LANES))
        band = pltpu.roll(wide, 0, 1, stride=1, stride_axis=0)[:, :OUT]
        for piece in range(SPLITS):
            part = band.astype(jnp.bfloat16)
            wbuf[piece, :, level * OUT : (level + 1) * OUT] = part
            band = band - part.astype(jnp.float32)


def details_of(main, halo, wbuf):
    ext = jnp.concatenate([main, halo], axis=1)
    windows = jnp.concatenate([ext[:, w * OUT : w * OUT + WIN] for w in range(NWIN)], axis=0)
    total = jnp.dot(windows, wbuf[0], preferred_element_type=jnp.float32)
    for piece in range(1, SPLITS):
        total += jnp.dot(windows, wbuf[piece], preferred_element_type=jnp.float32)
    return total.astype(jnp.bfloat16)


def kernel(
    p_ref, f_ref, o_ref,
    pbuf, hp, qbuf, hq, wbuf, dp, dq, part, sib, red, xo, yo, fin,
    hs, hr, xs, xr, xhs, xhr, cs, cr, chs, chr_, zus, zur, zds, zdr, zhus, zhur, zhds, zhdr,
    ss, sr, xos, xor_, yos, yor, fs, fr,
):
    a = lax.axis_index("tap")
    b = lax.axis_index("tm")
    y_hi = a // (NX * NZ)
    x = (a // NZ) % NX
    z = a % NZ
    y_lo = b // 2
    core = b % 2

    def tap_of(yh, xx, zz):
        return yh * (NX * NZ) + xx * NZ + zz

    b_next = (b + 1) % 8
    b_prev = (b + 7) % 8
    home = x % 2 == 0
    away = x % 2 == 1
    post = x // 2 == core
    far_tap = tap_of(1 - y_hi, 2 * (x // 2) + 1, z)
    z_up = tap_of(y_hi, x, (z + 1) % NZ)
    z_down = tap_of(y_hi, x, (z + NZ - 1) % NZ)
    sibling = y_lo * 2 + (1 - core)

    barrier = pltpu.get_barrier_semaphore()

    def hello(tap, tm):
        pl.semaphore_signal(barrier, inc=1, device_id=(tap, tm), device_id_type=MESH)

    hello(z_up, b)
    hello(z_down, b)
    hello(far_tap, b)

    @pl.when(away)
    def _():
        hello(tap_of(1 - y_hi, x - 1, z), b)

    hello(a, b_next)
    hello(a, b_prev)
    for d in range(1, 4):
        hello(a, (b + 2 * d) % 8)
        hello(tap_of(y_hi, (x + d) % NX, z), b)

    build_bands(f_ref, wbuf)
    pbuf[x] = p_ref[...]

    @pl.when(home)
    def _():
        qbuf[z, 0] = p_ref[...]

    pl.semaphore_wait(barrier, jnp.where(home, 11, 12))

    def far_copy(h):
        rows = pl.ds(h * HALF, HALF)
        return remote(
            p_ref.at[rows], qbuf.at[z, x % 2, rows], cs.at[h], cr.at[2 * (x % 2) + h], far_tap, b
        )

    sends = []

    def go(copy):
        copy.start()
        sends.append(copy)

    go(remote(p_ref.at[:, pl.ds(0, HALO)], hp.at[x], hs.at[0], hr.at[0], a, b_prev))
    for h in range(2):
        go(far_copy(h))
    for d in (3, 1, 2):
        go(remote(
            p_ref, pbuf.at[x], xs.at[d - 1], xr.at[d - 1], tap_of(y_hi, (x + d) % NX, z), b
        ))

    def chunk_of(zz, c):
        return qbuf.at[zz, c // 2, pl.ds((c % 2) * HALF, HALF)]

    def up(k, c):
        ref = chunk_of((z + NZ - k) % NZ, c)
        return remote(ref, ref, zus.at[4 * k + c], zur.at[4 * k + c], z_up, b)

    def down(k, c):
        ref = chunk_of((z + k) % NZ, c)
        return remote(ref, ref, zds.at[4 * k + c], zdr.at[4 * k + c], z_down, b)

    def from_below(k, c):
        ref = chunk_of((z + NZ - 1 - k) % NZ, c)
        remote(ref, ref, zus.at[4 * k + c], zur.at[4 * k + c], z_up, b).wait_recv()

    def from_above(k, c):
        ref = chunk_of((z + 1 + k) % NZ, c)
        remote(ref, ref, zds.at[4 * k + c], zdr.at[4 * k + c], z_down, b).wait_recv()

    def halo_up(k):
        zz = (z + NZ - k) % NZ
        ref = hq.at[zz] if k < 3 else hq.at[zz, 0]
        return remote(ref, ref, zhus.at[k], zhur.at[k], z_up, b)

    def halo_down(k):
        zz = (z + k) % NZ
        ref = hq.at[zz] if k < 3 else hq.at[zz, 1]
        return remote(ref, ref, zhds.at[k], zhdr.at[k], z_down, b)

    def halo_below(k):
        zz = (z + NZ - 1 - k) % NZ
        ref = hq.at[zz] if k < 3 else hq.at[zz, 0]
        remote(ref, ref, zhus.at[k], zhur.at[k], z_up, b).wait_recv()

    def halo_above(k):
        zz = (z + 1 + k) % NZ
        ref = hq.at[zz] if k < 3 else hq.at[zz, 1]
        remote(ref, ref, zhds.at[k], zhdr.at[k], z_down, b).wait_recv()

    def x_arrived(d):
        ref = pbuf.at[(x + NX - d) % NX]
        remote(ref, ref, xs.at[d - 1], xr.at[d - 1], z_up, b).wait_recv()

    @pl.when(home)
    def _():
        for c in range(2):
            up(0, c).start()
            down(0, c).start()

    remote(hp.at[x], hp.at[x], hs.at[0], hr.at[0], a, b_prev).wait_recv()
    for d in range(1, 4):
        go(remote(
            hp.at[x], hp.at[x], xhs.at[d - 1], xhr.at[d - 1], tap_of(y_hi, (x + d) % NX, z), b
        ))
    go(remote(hp.at[x], hq.at[z, x % 2], chs.at[0], chr_.at[x % 2], far_tap, b))
    x_arrived(3)

    @pl.when(home)
    def _():
        qbuf[z, 1] = pbuf[x + 1]
        for c in range(2, 4):
            up(0, c).start()
            down(0, c).start()

    @pl.when(away)
    def _():
        for c in range(4):
            ref = chunk_of(z, c)
            remote(ref, ref, cs.at[0], cr.at[c], far_tap, b).wait_recv()
            up(0, c).start()
            down(0, c).start()

    for c in range(4):
        sends.append(up(0, c))
        sends.append(down(0, c))
    x_arrived(1)
    x_arrived(2)
    for d in range(1, 4):
        ref = hp.at[(x + NX - d) % NX]
        remote(ref, ref, xhs.at[d - 1], xhr.at[d - 1], z_up, b).wait_recv()

    @pl.when(home)
    def _():
        hq[z, 0] = hp[x]
        hq[z, 1] = hp[x + 1]

    @pl.when(away)
    def _():
        for s in range(2):
            ref = hq.at[z, s]
            remote(ref, ref, chs.at[0], chr_.at[s], far_tap, b).wait_recv()

    go(halo_up(0))
    go(halo_down(0))

    val = details_of(
        jnp.concatenate([pbuf[i] for i in range(NX)], axis=0),
        jnp.concatenate([hp[i] for i in range(NX)], axis=0),
        wbuf,
    )
    for w in range(NWIN):
        for j in range(LEVELS):
            dp[j, :, w * OUT : (w + 1) * OUT] = val[
                w * NX * ROWS : (w + 1) * NX * ROWS, j * OUT : (j + 1) * OUT
            ]

    def columns(m):
        zz = (z + m) % NZ
        k, h = PIECE[m]
        val = details_of(
            jnp.concatenate([qbuf[zz, 0], qbuf[zz, 1]], axis=0),
            jnp.concatenate([hq[zz, 0], hq[zz, 1]], axis=0),
            wbuf,
        )
        for w in range(NWIN):
            for s in range(2):
                first = (2 * w + s) * ROWS
                to = s * 64 + h * ROWS
                for j in range(LEVELS):
                    dq[k, j, to : to + ROWS, w * OUT : (w + 1) * OUT] = (
                        val[first : first + ROWS, j * OUT : (j + 1) * OUT]
                    )

    def product(k):
        for j in range(LEVELS):
            prod = lax.dot_general(dp[j], dq[k, j], NT, preferred_element_type=jnp.float32)
            part[k, 0, j] = prod[0:64]
            part[k, 1, j] = prod[64:128]
        go(remote(part.at[k, 1 - core], sib.at[k], ss.at[k], sr.at[k], a, sibling))

    def x_copy(k, i):
        there = 2 * core + i
        d = (there - x + NX) % NX
        return remote(
            red.at[k, i], xo.at[k, x], xos.at[2 * k + i], xor_.at[3 * k + d - 1],
            tap_of(y_hi, there, z), b,
        )

    def x_out(k):
        ref = sib.at[k]
        remote(ref, ref, ss.at[k], sr.at[k], a, sibling).wait_recv()
        for i in range(2):
            red[k, i] = part[k, core, :, i * ROWS : (i + 1) * ROWS] + sib[k, :, i * ROWS : (i + 1) * ROWS]
            pl.when(2 * core + i != x)(lambda: x_copy(k, i).start())

        @pl.when(post)
        def _():
            xo[k, x] = red[k, x % 2]

    def x_for(t):
        return 2 * (t % 2) + jnp.where(t // 2 == y_hi, 0, 1)

    def y_copy(k, d):
        there = (y_lo + d) % NYL
        return remote(
            xo.at[k, x_for(there)], yo.at[k, d - 1], yos.at[3 * k + d - 1], yor.at[3 * k + d - 1],
            a, there * 2 + core,
        )

    def y_out(k):
        @pl.when(post)
        def _():
            for d in range(1, 4):
                ref = xo.at[k, (x + NX - d) % NX]
                remote(ref, ref, xos.at[0], xor_.at[3 * k + d - 1], z_up, b).wait_recv()
            for d in range(1, 4):
                y_copy(k, d).start()

    def fin_copy(k):
        return remote(fin.at[k], fin.at[k], fs.at[k], fr.at[k], a, sibling)

    def finish(k):
        @pl.when(post)
        def _():
            for d in range(1, 4):
                ref = yo.at[k, d - 1]
                remote(ref, ref, yos.at[0], yor.at[3 * k + d - 1], a, sibling).wait_recv()
            total = xo[k, x_for(y_lo)] + yo[k, 0] + yo[k, 1] + yo[k, 2]
            fin[k] = total * (1.0 / (WIDTH * 8))
            fin_copy(k).start()

    columns(0)
    for k in range(3):
        for c in range(4):
            from_below(k, c)
            if k < 2 or c < 2:
                go(up(k + 1, c))
            from_above(k, c)
            if k < 2 or c >= 2:
                go(down(k + 1, c))
            if c == 1 and k >= 1:
                x_out(k - 1)
        halo_below(k)
        go(halo_up(k + 1))
        halo_above(k)
        go(halo_down(k + 1))
        columns(1 + k)
        columns(7 - k)
        product(k)
        if k >= 2:
            y_out(k - 2)
    from_below(3, 0)
    from_above(3, 2)
    x_out(2)
    y_out(1)
    from_below(3, 1)
    from_above(3, 3)
    halo_below(3)
    halo_above(3)
    columns(4)
    product(3)
    x_out(3)
    y_out(2)
    finish(0)
    finish(1)
    y_out(3)
    finish(2)
    finish(3)

    @pl.when(jnp.logical_not(post))
    def _():
        for k in range(CHUNKS):
            fin_copy(k).wait_recv()

    group = lax.broadcasted_iota(jnp.int32, (ROWS, 128), 1) // ROWS
    for j in range(LEVELS):
        mine = []
        for k in range(CHUNKS):
            v = fin[k, j]
            mine.append(jnp.where(core == 0, v, pltpu.roll(v, 64, 1)))
        low = mine[3]
        high = pltpu.roll(mine[3], 96, 1)
        for k in range(3):
            low = jnp.where(group == k + 1, pltpu.roll(mine[k], 32 * (k + 1), 1), low)
            moved = mine[k] if k == 2 else pltpu.roll(mine[k], 64 - 32 * k, 1)
            high = jnp.where(group == 3 - k, moved, high)
        o_ref[j] = pltpu.roll(jnp.concatenate([low, high], axis=1), z * ROWS, 1)

    for copy in sends:
        copy.wait_send()
    for k in range(CHUNKS):
        for i in range(2):
            pl.when(2 * core + i != x)(lambda: x_copy(k, i).wait_send())

    @pl.when(post)
    def _():
        for k in range(CHUNKS):
            for d in range(1, 4):
                y_copy(k, d).wait_send()
            fin_copy(k).wait_send()


def body(pressure, filters):
    def sems(*counts):
        return [pltpu.SemaphoreType.DMA((n,)) for n in counts for _ in range(2)]

    f32, bf16 = jnp.float32, jnp.bfloat16
    return pl.pallas_call(
        kernel,
        out_shape=jax.ShapeDtypeStruct((LEVELS, ROWS, 256), f32),
        in_specs=[
            pl.BlockSpec(memory_space=pltpu.VMEM),
            pl.BlockSpec(memory_space=pltpu.SMEM),
        ],
        out_specs=pl.BlockSpec(memory_space=pltpu.VMEM),
        scratch_shapes=[
            pltpu.VMEM((NX, ROWS, WIDTH), bf16),
            pltpu.VMEM((NX, ROWS, HALO), bf16),
            pltpu.VMEM((NZ, 2, ROWS, WIDTH), bf16),
            pltpu.VMEM((NZ, 2, ROWS, HALO), bf16),
            pltpu.VMEM((SPLITS, WIN, LEVELS * OUT), bf16),
            pltpu.VMEM((LEVELS, NX * ROWS, WIDTH), bf16),
            pltpu.VMEM((CHUNKS, LEVELS, 128, WIDTH), bf16),
            pltpu.VMEM((CHUNKS, 2, LEVELS, 64, 128), f32),
            pltpu.VMEM((CHUNKS, LEVELS, 64, 128), f32),
            pltpu.VMEM((CHUNKS, 2, LEVELS, ROWS, 128), f32),
            pltpu.VMEM((CHUNKS, NX, LEVELS, ROWS, 128), f32),
            pltpu.VMEM((CHUNKS, 3, LEVELS, ROWS, 128), f32),
            pltpu.VMEM((CHUNKS, LEVELS, ROWS, 128), f32),
            *sems(1, 3, 3, 4, 2, 16, 16, 4, 4, CHUNKS, 3 * CHUNKS, 3 * CHUNKS, CHUNKS),
        ],
        compiler_params=pltpu.CompilerParams(
            collective_id=0, has_side_effects=True, vmem_limit_bytes=40 * 1024 * 1024
        ),
        cost_estimate=pl.CostEstimate(
            flops=4_000_000_000, bytes_accessed=200_000, transcendentals=0
        ),
    )(pressure, filters)


def solution(mesh):
    placed = (P("tap", "tm"), P())
    return jax.shard_map(
        body, mesh=mesh, in_specs=placed, out_specs=P(None, "tap", "tm"), check_vma=False
    )
```

```python
import jax
import jax.numpy as jnp
from jax import lax
from jax.experimental import pallas as pl
from jax.experimental.pallas import tpu as pltpu
from jax.sharding import PartitionSpec as P

FILT = 16
LEVELS = 3
NX, NZ, NYL = 4, 8, 4
ROWS = 32
WIDTH = 1024
HALO = 128
WIN = 256
OUT = 128
NWIN = WIDTH // OUT
SPLITS = 3
LANES = 384
CHUNKS = 4
HALF = 16
MESH = pl.DeviceIdType.MESH
NT = (((1,), (1,)), ((), ()))


def remote(src, dst, send, recv, tap, tm):
    return pltpu.make_async_remote_copy(
        src_ref=src, dst_ref=dst, send_sem=send, recv_sem=recv,
        device_id=(tap, tm), device_id_type=MESH,
    )


def build_bands(f_ref, wbuf):
    lane = lax.broadcasted_iota(jnp.int32, (8, LANES), 1)

    def comb(row, top, step):
        line = jnp.zeros((8, LANES), jnp.float32)
        for k in range(FILT):
            line = jnp.where(lane == top - step * k, f_ref[row, k], line)
        return line

    def smoothed(line, step):
        total = jnp.zeros((8, LANES), jnp.float32)
        for k in range(FILT):
            moved = line if k == 0 else pltpu.roll(line, LANES - step * k, 1)
            total = total + f_ref[1, k] * moved
        return total

    lines = [
        comb(0, 328, 1),
        smoothed(comb(0, 344, 2), 1),
        smoothed(smoothed(comb(0, 376, 4), 2), 1),
    ]
    for level, line in enumerate(lines):
        wide = jnp.broadcast_to(line[0:1, :], (WIN, LANES))
        band = pltpu.roll(wide, 0, 1, stride=1, stride_axis=0)[:, :OUT]
        for piece in range(SPLITS):
            part = band.astype(jnp.bfloat16)
            wbuf[piece, :, level * OUT : (level + 1) * OUT] = part
            band = band - part.astype(jnp.float32)


def details_of(main, halo, wbuf):
    ext = jnp.concatenate([main, halo], axis=1)
    windows = jnp.concatenate([ext[:, w * OUT : w * OUT + WIN] for w in range(NWIN)], axis=0)
    total = jnp.dot(windows, wbuf[0], preferred_element_type=jnp.float32)
    for piece in range(1, SPLITS):
        total += jnp.dot(windows, wbuf[piece], preferred_element_type=jnp.float32)
    return total.astype(jnp.bfloat16)


def kernel(
    p_ref, f_ref, o_ref,
    pbuf, hp, qbuf, hq, wbuf, dp, dq, part, sib, red, xo, yo,
    ps, hs, hr, xs, xr, xhs, xhr, cs, cr, chs, chr_, zus, zur, zds, zdr, zhs, zhr,
    ss, sr, xos, xor_, yos, yor,
):
    a = lax.axis_index("tap")
    b = lax.axis_index("tm")
    y_hi = a // (NX * NZ)
    x = (a // NZ) % NX
    z = a % NZ
    y_lo = b // 2
    core = b % 2

    def tap_of(yh, xx, zz):
        return yh * (NX * NZ) + xx * NZ + zz

    b_next = (b + 1) % 8
    b_prev = (b + 7) % 8
    post = x % 2 == core
    far_tap = tap_of(1 - y_hi, x, z)
    z_up = tap_of(y_hi, x, (z + 1) % NZ)
    z_down = tap_of(y_hi, x, (z + NZ - 1) % NZ)
    sibling = y_lo * 2 + (1 - core)

    fetch = pltpu.make_async_copy(p_ref, pbuf.at[x], ps.at[0])
    fetch.start()
    barrier = pltpu.get_barrier_semaphore()

    def hello(tap, tm):
        pl.semaphore_signal(barrier, inc=1, device_id=(tap, tm), device_id_type=MESH)

    for d in (1, 7, 2, 6, 3, 5, 4):
        hello(tap_of(y_hi, x, (z + d) % NZ), b)
    hello(far_tap, b)
    hello(a, b_next)
    hello(a, b_prev)
    for d in range(1, 4):
        hello(a, (b + 2 * d) % 8)
        hello(tap_of(y_hi, (x + d) % NX, z), b)

    build_bands(f_ref, wbuf)
    fetch.wait()
    pl.semaphore_wait(barrier, 16)

    sends = []

    def go(copy):
        copy.start()
        sends.append(copy)

    def rows_of(c):
        return pl.ds(c * HALF, HALF)

    def up(t, k, c):
        dst = qbuf.at[t, (z + NZ - k) % NZ, rows_of(c)]
        src = pbuf.at[x, rows_of(c)] if t == 0 and k == 0 else dst
        n = 8 * t + 2 * k + c
        return remote(src, dst, zus.at[n], zur.at[n], z_up, b)

    def down(t, k, c):
        dst = qbuf.at[t, (z + k) % NZ, rows_of(c)]
        src = pbuf.at[x, rows_of(c)] if t == 0 and k == 0 else dst
        n = 8 * t + 2 * k + c
        return remote(src, dst, zds.at[n], zdr.at[n], z_down, b)

    def from_below(t, k, c):
        ref = qbuf.at[t, (z + NZ - 1 - k) % NZ, rows_of(c)]
        n = 8 * t + 2 * k + c
        remote(ref, ref, zus.at[n], zur.at[n], z_up, b).wait_recv()

    def from_above(t, k, c):
        ref = qbuf.at[t, (z + 1 + k) % NZ, rows_of(c)]
        n = 8 * t + 2 * k + c
        remote(ref, ref, zds.at[n], zdr.at[n], z_down, b).wait_recv()

    def far(m, c):
        zz = (z + m) % NZ
        src = pbuf.at[x, rows_of(c)] if m == 0 else qbuf.at[0, zz, rows_of(c)]
        n = (2 if m else 0) + c
        return remote(src, qbuf.at[1, zz, rows_of(c)], cs.at[n], cr.at[n], far_tap, b)

    def from_far(m, c):
        ref = qbuf.at[1, (z + m) % NZ, rows_of(c)]
        n = (2 if m else 0) + c
        remote(ref, ref, cs.at[n], cr.at[n], far_tap, b).wait_recv()

    def send_halos(t):
        src = hp.at[x] if t == 0 else hq.at[1, z]
        for d in (1, 7, 2, 6, 3, 5, 4):
            n = 7 * t + d - 1
            go(remote(
                src, hq.at[t, z], zhs.at[n], zhr.at[n], tap_of(y_hi, x, (z + d) % NZ), b
            ))

    def halo_from(t, m):
        ref = hq.at[t, (z + m) % NZ]
        n = 7 * t + (NZ - m) - 1
        remote(ref, ref, zhs.at[n], zhr.at[n], z_up, b).wait_recv()

    def step(t, k):
        for c in range(2):
            from_below(t, k, c)
            if k < 2 or (t == 0 and c == 0):
                go(up(t, k + 1, c))
            from_above(t, k, c)
            if k < 2 or (t == 0 and c == 1):
                go(down(t, k + 1, c))

    def columns(t, *places):
        for m in places:
            if m:
                halo_from(t, m)
        val = details_of(
            jnp.concatenate([qbuf[t, (z + m) % NZ] for m in places], axis=0),
            jnp.concatenate([hq[t, (z + m) % NZ] for m in places], axis=0),
            wbuf,
        )
        for w in range(NWIN):
            for n, m in enumerate(places):
                first = (len(places) * w + n) * ROWS
                q, to = 2 * t + (m + 1) % NZ // 4, (m + 1) % 4 * ROWS
                for j in range(LEVELS):
                    dq[q, j, to : to + ROWS, w * OUT : (w + 1) * OUT] = (
                        val[first : first + ROWS, j * OUT : (j + 1) * OUT]
                    )

    def sib_copy(q):
        return remote(part.at[q], sib.at[q], ss.at[q], sr.at[q], a, sibling)

    def product(q):
        for j in range(LEVELS):
            part[q, j] = lax.dot_general(dp[j], dq[q, j], NT, preferred_element_type=jnp.float32)
        pl.when(jnp.logical_not(post))(lambda: sib_copy(q).start())

    def x_copy(q, d):
        there = (x + d) % NX
        return remote(
            red.at[q, there], xo.at[q, x // 2], xos.at[3 * q + d - 1], xor_.at[2 * q + x // 2],
            tap_of(y_hi, there, z), b,
        )

    def x_out(q):
        @pl.when(post)
        def _():
            sib_copy(q).wait_recv()
            for i in range(NX):
                rows = slice(i * ROWS, (i + 1) * ROWS)
                red[q, i] = part[q, :, rows] + sib[q, :, rows]
            for d in (2, 1, 3):
                x_copy(q, d).start()
            xo[q, x // 2] = red[q, x]

    def y_goal(q, i):
        return 2 * (y_hi if q < 2 else 1 - y_hi) + i

    def y_copy(q, i):
        goal = y_goal(q, i)
        d = (goal - y_lo + NYL) % NYL
        n = 3 * (q % 2) + d - 1
        return remote(
            xo.at[q, i], yo.at[q % 2, d - 1], yos.at[2 * q + i], yor.at[n], a, goal * 2 + core
        )

    def y_out(q):
        for i in range(2):
            @pl.when(2 * i + core != x)
            def _():
                ref = xo.at[q, i]
                remote(ref, ref, xos.at[0], xor_.at[2 * q + i], z_up, b).wait_recv()

            pl.when(y_goal(q, i) != y_lo)(lambda: y_copy(q, i).start())

    for c in range(2):
        go(far(0, c))
    go(remote(pbuf.at[x, :, pl.ds(0, HALO)], hp.at[x], hs.at[0], hr.at[0], a, b_prev))
    for c in range(2):
        go(up(0, 0, c))
        go(down(0, 0, c))
    for d in range(1, 4):
        go(remote(
            pbuf.at[x], pbuf.at[x], xs.at[d - 1], xr.at[d - 1], tap_of(y_hi, (x + d) % NX, z), b
        ))

    step(0, 0)
    remote(hp.at[x], hp.at[x], hs.at[0], hr.at[0], a, b_prev).wait_recv()
    go(remote(hp.at[x], hq.at[1, z], chs.at[0], chr_.at[0], far_tap, b))
    for d in range(1, 4):
        go(remote(
            hp.at[x], hp.at[x], xhs.at[d - 1], xhr.at[d - 1], tap_of(y_hi, (x + d) % NX, z), b
        ))
    send_halos(0)
    for d in range(1, 4):
        ref = pbuf.at[(x + NX - d) % NX]
        remote(ref, ref, xs.at[d - 1], xr.at[d - 1], z_up, b).wait_recv()
    step(0, 1)
    for c in range(2):
        from_far(0, c)
        go(up(1, 0, c))
        go(down(1, 0, c))
    for d in range(1, 4):
        ref = hp.at[(x + NX - d) % NX]
        remote(ref, ref, xhs.at[d - 1], xhr.at[d - 1], z_up, b).wait_recv()
    val = details_of(
        jnp.concatenate([pbuf[i] for i in range(NX)], axis=0),
        jnp.concatenate([hp[i] for i in range(NX)], axis=0),
        wbuf,
    )
    for w in range(NWIN):
        for j in range(LEVELS):
            dp[j, :, w * OUT : (w + 1) * OUT] = val[
                w * NX * ROWS : (w + 1) * NX * ROWS, j * OUT : (j + 1) * OUT
            ]
    own = pl.ds(pl.multiple_of(x * ROWS, ROWS), ROWS)
    for j in range(LEVELS):
        dq[0, j, ROWS : 2 * ROWS] = dp[j, own, :]
    remote(hq.at[1, z], hq.at[1, z], chs.at[0], chr_.at[0], far_tap, b).wait_recv()
    send_halos(1)
    columns(0, 1, 7)
    step(0, 2)
    columns(0, 2, 6)
    product(0)
    step(1, 0)
    from_below(0, 3, 0)
    go(far(4, 0))
    from_above(0, 3, 1)
    go(far(4, 1))
    x_out(0)
    columns(0, 3, 5)
    columns(0, 4)
    product(1)
    step(1, 1)
    columns(1, 0, 1)
    columns(1, 7, 2)
    product(2)
    x_out(1)
    y_out(0)
    columns(1, 6)
    x_out(2)
    step(1, 2)
    columns(1, 3, 5)
    y_out(1)
    for c in range(2):
        from_far(4, c)
    columns(1, 4)
    product(3)
    y_out(2)
    x_out(3)
    y_out(3)

    kind = jnp.where(y_lo // 2 == y_hi, 0, 2)
    totals = []
    for h in range(2):
        for d in range(1, 4):
            ref = yo.at[h, d - 1]
            remote(ref, ref, yos.at[0], yor.at[3 * h + d - 1], a, sibling).wait_recv()
        totals.append(xo[kind + h, y_lo % 2] + yo[h, 0] + yo[h, 1] + yo[h, 2])
    total = jnp.concatenate(totals, axis=2) * (1.0 / (WIDTH * 8))
    for j in range(LEVELS):
        o_ref[j] = pltpu.roll(total[j], ((z + NZ - 1) % NZ) * ROWS, 1)

    for copy in sends:
        copy.wait_send()
    for q in range(CHUNKS):
        @pl.when(post)
        def _():
            for d in range(1, 4):
                x_copy(q, d).wait_send()

        pl.when(jnp.logical_not(post))(lambda: sib_copy(q).wait_send())
        for i in range(2):
            pl.when(y_goal(q, i) != y_lo)(lambda: y_copy(q, i).wait_send())


def body(pressure, filters):
    def sems(*counts):
        return [pltpu.SemaphoreType.DMA((n,)) for n in counts for _ in range(2)]

    f32, bf16 = jnp.float32, jnp.bfloat16
    return pl.pallas_call(
        kernel,
        out_shape=jax.ShapeDtypeStruct((LEVELS, ROWS, 256), f32),
        in_specs=[
            pl.BlockSpec(memory_space=pltpu.HBM),
            pl.BlockSpec(memory_space=pltpu.SMEM),
        ],
        out_specs=pl.BlockSpec(memory_space=pltpu.VMEM),
        scratch_shapes=[
            pltpu.VMEM((NX, ROWS, WIDTH), bf16),
            pltpu.VMEM((NX, ROWS, HALO), bf16),
            pltpu.VMEM((2, NZ, ROWS, WIDTH), bf16),
            pltpu.VMEM((2, NZ, ROWS, HALO), bf16),
            pltpu.VMEM((SPLITS, WIN, LEVELS * OUT), bf16),
            pltpu.VMEM((LEVELS, NX * ROWS, WIDTH), bf16),
            pltpu.VMEM((CHUNKS, LEVELS, 128, WIDTH), bf16),
            pltpu.VMEM((CHUNKS, LEVELS, NX * ROWS, 128), f32),
            pltpu.VMEM((CHUNKS, LEVELS, NX * ROWS, 128), f32),
            pltpu.VMEM((CHUNKS, NX, LEVELS, ROWS, 128), f32),
            pltpu.VMEM((CHUNKS, 2, LEVELS, ROWS, 128), f32),
            pltpu.VMEM((2, 3, LEVELS, ROWS, 128), f32),
            pltpu.SemaphoreType.DMA((1,)),
            *sems(1, 3, 3, 4, 1, 16, 16, 14, CHUNKS, 3 * CHUNKS, 2 * CHUNKS),
        ],
        compiler_params=pltpu.CompilerParams(
            collective_id=0, has_side_effects=True, vmem_limit_bytes=40 * 1024 * 1024
        ),
        cost_estimate=pl.CostEstimate(
            flops=4_000_000_000, bytes_accessed=200_000, transcendentals=0
        ),
    )(pressure, filters)


def solution(mesh):
    placed = (P("tap", "tm"), P())
    return jax.shard_map(
        body, mesh=mesh, in_specs=placed, out_specs=P(None, "tap", "tm"), check_vma=False
    )
```

```python
import jax
import jax.numpy as jnp
from jax import lax
from jax.experimental import pallas as pl
from jax.experimental.pallas import tpu as pltpu
from jax.sharding import PartitionSpec as P

FILT = 16
LEVELS = 3
NX, NZ, NYL = 4, 8, 4
ROWS = 32
WIDTH = 1024
HALO = 128
WIN = 256
OUT = 128
NWIN = WIDTH // OUT
SPLITS = 3
LANES = 384
CHUNKS = 4
HALF = 16
HOPS = ((0, 2, 0), (0, 2, 1), (0, 1, 2), (2, 1, 0), (2, 1, 1), (2, 2, None))
MESH = pl.DeviceIdType.MESH
NT = (((1,), (1,)), ((), ()))


def remote(src, dst, send, recv, tap, tm):
    return pltpu.make_async_remote_copy(
        src_ref=src, dst_ref=dst, send_sem=send, recv_sem=recv,
        device_id=(tap, tm), device_id_type=MESH,
    )


def build_bands(f_ref, wbuf):
    lane = lax.broadcasted_iota(jnp.int32, (8, LANES), 1)

    def comb(row, top, step):
        line = jnp.zeros((8, LANES), jnp.float32)
        for k in range(FILT):
            line = jnp.where(lane == top - step * k, f_ref[row, k], line)
        return line

    def smoothed(line, step):
        total = jnp.zeros((8, LANES), jnp.float32)
        for k in range(FILT):
            moved = line if k == 0 else pltpu.roll(line, LANES - step * k, 1)
            total = total + f_ref[1, k] * moved
        return total

    lines = [
        comb(0, 328, 1),
        smoothed(comb(0, 344, 2), 1),
        smoothed(smoothed(comb(0, 376, 4), 2), 1),
    ]
    for level, line in enumerate(lines):
        wide = jnp.broadcast_to(line[0:1, :], (WIN, LANES))
        band = pltpu.roll(wide, 0, 1, stride=1, stride_axis=0)[:, :OUT]
        for piece in range(SPLITS):
            part = band.astype(jnp.bfloat16)
            wbuf[piece, :, level * OUT : (level + 1) * OUT] = part
            band = band - part.astype(jnp.float32)


def details_of(main, halo, wbuf):
    ext = jnp.concatenate([main, halo], axis=1)
    windows = jnp.concatenate([ext[:, w * OUT : w * OUT + WIN] for w in range(NWIN)], axis=0)
    total = jnp.dot(windows, wbuf[0], preferred_element_type=jnp.float32)
    for piece in range(1, SPLITS):
        total += jnp.dot(windows, wbuf[piece], preferred_element_type=jnp.float32)
    return total.astype(jnp.bfloat16)


def kernel(
    p_ref, f_ref, o_ref,
    pbuf, hp, qbuf, hq, wbuf, dp, dq, part, sib, red, xo, yo,
    ps, hs, hr, xs, xr, xhs, xhr, cs, cr, chs, chr_, zs, zr, zhs, zhr, ths, thr,
    ss, sr, xos, xor_, yos, yor,
):
    a = lax.axis_index("tap")
    b = lax.axis_index("tm")
    y_hi = a // (NX * NZ)
    x = (a // NZ) % NX
    z = a % NZ
    y_lo = b // 2
    core = b % 2

    def tap_of(yh, xx, zz):
        return yh * (NX * NZ) + xx * NZ + zz

    b_next = (b + 1) % 8
    b_prev = (b + 7) % 8
    post = x % 2 == core
    far_tap = tap_of(1 - y_hi, x, z)
    z_up = tap_of(y_hi, x, (z + 1) % NZ)
    sibling = y_lo * 2 + (1 - core)

    fetch = pltpu.make_async_copy(p_ref, pbuf.at[x], ps.at[0])
    fetch.start()
    barrier = pltpu.get_barrier_semaphore()

    def hello(tap, tm):
        pl.semaphore_signal(barrier, inc=1, device_id=(tap, tm), device_id_type=MESH)

    for d in (1, 7, 2, 6, 3, 5, 4):
        hello(tap_of(y_hi, x, (z + d) % NZ), b)
    hello(far_tap, b)
    hello(a, b_next)
    hello(a, b_prev)
    for d in range(1, 4):
        hello(a, (b + 2 * d) % 8)
        hello(tap_of(y_hi, (x + d) % NX, z), b)

    build_bands(f_ref, wbuf)
    fetch.wait()
    pl.semaphore_wait(barrier, 16)

    sends = []

    def go(copy):
        copy.start()
        sends.append(copy)

    def rows_of(c):
        return pl.ds(c * HALF, HALF)

    def hop(t, way, n):
        behind, dist, rows = HOPS[n]
        if rows is None:
            rows = 0 if way == 1 else 1
        span = pl.ds(0, ROWS) if rows == 2 else rows_of(rows)
        slot = (z + NZ - way * behind) % NZ
        dst = qbuf.at[t, slot, span]
        src = pbuf.at[x, span] if t == 0 and behind == 0 else dst
        i = (6 * t + n) * 2 + (way + 1) // 2
        return remote(
            src, dst, zs.at[i], zr.at[i], tap_of(y_hi, x, (z + NZ + way * dist) % NZ), b
        )

    def arrived(t, way, n):
        behind, dist, rows = HOPS[n]
        if rows is None:
            rows = 0 if way == 1 else 1
        span = pl.ds(0, ROWS) if rows == 2 else rows_of(rows)
        ref = qbuf.at[t, (z + NZ - way * (behind + dist)) % NZ, span]
        i = (6 * t + n) * 2 + (way + 1) // 2
        remote(ref, ref, zs.at[i], zr.at[i], z_up, b).wait_recv()

    def first_hops(t, *ns):
        for n in ns:
            for way in (1, -1):
                go(hop(t, way, n))

    def pass_on(t):
        for c in range(2):
            for way in (1, -1):
                arrived(t, way, c)
                if t == 0 and c == (1 - way) // 2:
                    go(hop(t, way, 5))
                go(hop(t, way, 3 + c))
        if t == 0:
            go(later_halo(6))
            go(later_halo(2))

    def wait_for(t, *ns):
        for n in ns:
            for way in (1, -1):
                arrived(t, way, n)

    def far(m, c):
        zz = (z + m) % NZ
        src = pbuf.at[x, rows_of(c)] if m == 0 else qbuf.at[0, zz, rows_of(c)]
        n = (2 if m else 0) + c
        return remote(src, qbuf.at[1, zz, rows_of(c)], cs.at[n], cr.at[n], far_tap, b)

    def from_far(m, c):
        ref = qbuf.at[1, (z + m) % NZ, rows_of(c)]
        n = (2 if m else 0) + c
        remote(ref, ref, cs.at[n], cr.at[n], far_tap, b).wait_recv()

    def owner_halo(m):
        d = NZ - m
        return remote(
            hq.at[1, z], hq.at[1, z], zhs.at[d - 1], zhr.at[d - 1],
            tap_of(y_hi, x, (z + d) % NZ), b,
        )

    def later_halo(m):
        zz = (z + m) % NZ
        return remote(
            qbuf.at[0, zz, :, pl.ds(0, HALO)], hq.at[0, zz], ths.at[m], thr.at[m], a, b_prev
        )

    def halo_from(t, m):
        if t == 1:
            ref = hq.at[1, (z + m) % NZ]
            remote(ref, ref, zhs.at[NZ - m - 1], zhr.at[NZ - m - 1], z_up, b).wait_recv()
        else:
            later_halo(m).wait_recv()

    def columns(t, *places):
        for m in places:
            if m:
                halo_from(t, m)
        val = details_of(
            jnp.concatenate([qbuf[t, (z + m) % NZ] for m in places], axis=0),
            jnp.concatenate([hq[t, (z + m) % NZ] for m in places], axis=0),
            wbuf,
        )
        for w in range(NWIN):
            for n, m in enumerate(places):
                first = (len(places) * w + n) * ROWS
                q, to = 2 * t + (m + 1) % NZ // 4, (m + 1) % 4 * ROWS
                for j in range(LEVELS):
                    dq[q, j, to : to + ROWS, w * OUT : (w + 1) * OUT] = (
                        val[first : first + ROWS, j * OUT : (j + 1) * OUT]
                    )

    def sib_copy(q):
        return remote(part.at[q], sib.at[q], ss.at[q], sr.at[q], a, sibling)

    def product(q):
        for j in range(LEVELS):
            part[q, j] = lax.dot_general(dp[j], dq[q, j], NT, preferred_element_type=jnp.float32)
        pl.when(jnp.logical_not(post))(lambda: sib_copy(q).start())

    def x_copy(q, d):
        there = (x + d) % NX
        return remote(
            red.at[q, there], xo.at[q, x // 2], xos.at[3 * q + d - 1], xor_.at[2 * q + x // 2],
            tap_of(y_hi, there, z), b,
        )

    def x_out(q):
        @pl.when(post)
        def _():
            sib_copy(q).wait_recv()
            for i in range(NX):
                rows = slice(i * ROWS, (i + 1) * ROWS)
                red[q, i] = part[q, :, rows] + sib[q, :, rows]
            for d in (2, 1, 3):
                x_copy(q, d).start()
            xo[q, x // 2] = red[q, x]

    def y_goal(q, i):
        return 2 * (y_hi if q < 2 else 1 - y_hi) + i

    def y_copy(q, i):
        goal = y_goal(q, i)
        d = (goal - y_lo + NYL) % NYL
        n = 3 * (q % 2) + d - 1
        return remote(
            xo.at[q, i], yo.at[q % 2, d - 1], yos.at[2 * q + i], yor.at[n], a, goal * 2 + core
        )

    def y_out(q):
        for i in range(2):
            @pl.when(2 * i + core != x)
            def _():
                ref = xo.at[q, i]
                remote(ref, ref, xos.at[0], xor_.at[2 * q + i], z_up, b).wait_recv()

            pl.when(y_goal(q, i) != y_lo)(lambda: y_copy(q, i).start())

    for c in range(2):
        go(far(0, c))
    go(remote(pbuf.at[x, :, pl.ds(0, HALO)], hp.at[x], hs.at[0], hr.at[0], a, b_prev))
    first_hops(0, 0, 1)
    for d in range(1, 4):
        go(remote(
            pbuf.at[x], pbuf.at[x], xs.at[d - 1], xr.at[d - 1], tap_of(y_hi, (x + d) % NX, z), b
        ))
    first_hops(0, 2)

    remote(hp.at[x], hp.at[x], hs.at[0], hr.at[0], a, b_prev).wait_recv()
    go(remote(hp.at[x], hq.at[1, z], chs.at[0], chr_.at[0], far_tap, b))
    for d in range(1, 4):
        go(remote(
            hp.at[x], hp.at[x], xhs.at[d - 1], xhr.at[d - 1], tap_of(y_hi, (x + d) % NX, z), b
        ))
    pass_on(0)
    for c in range(2):
        from_far(0, c)
        first_hops(1, c)
    first_hops(1, 2)
    wait_for(0, 2)
    go(later_halo(1))
    go(later_halo(7))
    for d in range(1, 4):
        ref = pbuf.at[(x + NX - d) % NX]
        remote(ref, ref, xs.at[d - 1], xr.at[d - 1], z_up, b).wait_recv()
    for d in range(1, 4):
        ref = hp.at[(x + NX - d) % NX]
        remote(ref, ref, xhs.at[d - 1], xhr.at[d - 1], z_up, b).wait_recv()
    val = details_of(
        jnp.concatenate([pbuf[i] for i in range(NX)], axis=0),
        jnp.concatenate([hp[i] for i in range(NX)], axis=0),
        wbuf,
    )
    for w in range(NWIN):
        for j in range(LEVELS):
            dp[j, :, w * OUT : (w + 1) * OUT] = val[
                w * NX * ROWS : (w + 1) * NX * ROWS, j * OUT : (j + 1) * OUT
            ]
    own = pl.ds(pl.multiple_of(x * ROWS, ROWS), ROWS)
    for j in range(LEVELS):
        dq[0, j, ROWS : 2 * ROWS] = dp[j, own, :]
    remote(hq.at[1, z], hq.at[1, z], chs.at[0], chr_.at[0], far_tap, b).wait_recv()
    for m in (2, 6, 1, 7, 3, 5, 4):
        go(owner_halo(m))
    columns(0, 2, 6)
    columns(0, 1, 7)
    product(0)
    for c in range(2):
        arrived(0, 1 - 2 * c, 5)
        go(far(4, c))
    go(later_halo(4))
    wait_for(0, 3, 4)
    go(later_halo(3))
    go(later_halo(5))
    pass_on(1)
    x_out(0)
    wait_for(1, 2)
    columns(1, 0, 2)
    columns(1, 1, 7)
    product(2)
    columns(0, 3, 5)
    columns(0, 4)
    product(1)
    x_out(2)
    columns(1, 6)
    y_out(0)
    x_out(1)
    wait_for(1, 3, 4)
    columns(1, 3, 5)
    for c in range(2):
        from_far(4, c)
    columns(1, 4)
    product(3)
    x_out(3)
    y_out(2)
    y_out(1)
    y_out(3)

    kind = jnp.where(y_lo // 2 == y_hi, 0, 2)
    totals = []
    for h in range(2):
        for d in range(1, 4):
            ref = yo.at[h, d - 1]
            remote(ref, ref, yos.at[0], yor.at[3 * h + d - 1], a, sibling).wait_recv()
        totals.append(xo[kind + h, y_lo % 2] + yo[h, 0] + yo[h, 1] + yo[h, 2])
    total = jnp.concatenate(totals, axis=2) * (1.0 / (WIDTH * 8))
    for j in range(LEVELS):
        o_ref[j] = pltpu.roll(total[j], ((z + NZ - 1) % NZ) * ROWS, 1)

    for copy in sends:
        copy.wait_send()
    for q in range(CHUNKS):
        @pl.when(post)
        def _():
            for d in range(1, 4):
                x_copy(q, d).wait_send()

        pl.when(jnp.logical_not(post))(lambda: sib_copy(q).wait_send())
        for i in range(2):
            pl.when(y_goal(q, i) != y_lo)(lambda: y_copy(q, i).wait_send())


def body(pressure, filters):
    def sems(*counts):
        return [pltpu.SemaphoreType.DMA((n,)) for n in counts for _ in range(2)]

    f32, bf16 = jnp.float32, jnp.bfloat16
    return pl.pallas_call(
        kernel,
        out_shape=jax.ShapeDtypeStruct((LEVELS, ROWS, 256), f32),
        in_specs=[
            pl.BlockSpec(memory_space=pltpu.HBM),
            pl.BlockSpec(memory_space=pltpu.SMEM),
        ],
        out_specs=pl.BlockSpec(memory_space=pltpu.VMEM),
        scratch_shapes=[
            pltpu.VMEM((NX, ROWS, WIDTH), bf16),
            pltpu.VMEM((NX, ROWS, HALO), bf16),
            pltpu.VMEM((2, NZ, ROWS, WIDTH), bf16),
            pltpu.VMEM((2, NZ, ROWS, HALO), bf16),
            pltpu.VMEM((SPLITS, WIN, LEVELS * OUT), bf16),
            pltpu.VMEM((LEVELS, NX * ROWS, WIDTH), bf16),
            pltpu.VMEM((CHUNKS, LEVELS, 128, WIDTH), bf16),
            pltpu.VMEM((CHUNKS, LEVELS, NX * ROWS, 128), f32),
            pltpu.VMEM((CHUNKS, LEVELS, NX * ROWS, 128), f32),
            pltpu.VMEM((CHUNKS, NX, LEVELS, ROWS, 128), f32),
            pltpu.VMEM((CHUNKS, 2, LEVELS, ROWS, 128), f32),
            pltpu.VMEM((2, 3, LEVELS, ROWS, 128), f32),
            pltpu.SemaphoreType.DMA((1,)),
            *sems(1, 3, 3, 4, 1, 24, 7, 8, CHUNKS, 3 * CHUNKS, 2 * CHUNKS),
        ],
        compiler_params=pltpu.CompilerParams(
            collective_id=0, has_side_effects=True, vmem_limit_bytes=40 * 1024 * 1024
        ),
        cost_estimate=pl.CostEstimate(
            flops=4_000_000_000, bytes_accessed=200_000, transcendentals=0
        ),
    )(pressure, filters)


def solution(mesh):
    placed = (P("tap", "tm"), P())
    return jax.shard_map(
        body, mesh=mesh, in_specs=placed, out_specs=P(None, "tap", "tm"), check_vma=False
    )
```

```python
import jax
import jax.numpy as jnp
from jax import lax
from jax.experimental import pallas as pl
from jax.experimental.pallas import tpu as pltpu
from jax.sharding import PartitionSpec as P

FILT = 16
LEVELS = 3
NX, NZ, NYL = 4, 8, 4
ROWS = 32
WIDTH = 1024
HALO = 128
WIN = 256
OUT = 128
NWIN = WIDTH // OUT
SPLITS = 2
LANES = 384
CHUNKS = 4
HALF = 16
HOPS = ((0, 2, 0), (0, 2, 1), (0, 1, 2), (2, 1, 0), (2, 1, 1), (2, 2, None))
MESH = pl.DeviceIdType.MESH
NT = (((1,), (1,)), ((), ()))


def remote(src, dst, send, recv, tap, tm):
    return pltpu.make_async_remote_copy(
        src_ref=src, dst_ref=dst, send_sem=send, recv_sem=recv,
        device_id=(tap, tm), device_id_type=MESH,
    )


def build_bands(f_ref, wbuf):
    lane = lax.broadcasted_iota(jnp.int32, (8, LANES), 1)

    def comb(row, top, step):
        line = jnp.zeros((8, LANES), jnp.float32)
        for k in range(FILT):
            line = jnp.where(lane == top - step * k, f_ref[row, k], line)
        return line

    def smoothed(line, step):
        total = jnp.zeros((8, LANES), jnp.float32)
        for k in range(FILT):
            moved = line if k == 0 else pltpu.roll(line, LANES - step * k, 1)
            total = total + f_ref[1, k] * moved
        return total

    lines = [
        comb(0, 328, 1),
        smoothed(comb(0, 344, 2), 1),
        smoothed(smoothed(comb(0, 376, 4), 2), 1),
    ]
    for level, line in enumerate(lines):
        wide = jnp.broadcast_to(line[0:1, :], (WIN, LANES))
        band = pltpu.roll(wide, 0, 1, stride=1, stride_axis=0)[:, :OUT]
        for piece in range(SPLITS):
            part = band.astype(jnp.bfloat16)
            wbuf[piece, :, level * OUT : (level + 1) * OUT] = part
            band = band - part.astype(jnp.float32)


def details_of(main, halo, wbuf):
    ext = jnp.concatenate([main, halo], axis=1)
    windows = jnp.concatenate([ext[:, w * OUT : w * OUT + WIN] for w in range(NWIN)], axis=0)
    total = jnp.dot(windows, wbuf[0], preferred_element_type=jnp.float32)
    for piece in range(1, SPLITS):
        total += jnp.dot(windows, wbuf[piece], preferred_element_type=jnp.float32)
    return total.astype(jnp.bfloat16)


def kernel(
    p_ref, f_hbm, o_ref,
    f_ref, pbuf, hp, qbuf, hq, wbuf, dp, dq, part, sib, red, xo, yo,
    ps, hs, hr, xs, xr, xhs, xhr, cs, cr, chs, chr_, zs, zr, zhs, zhr, ths, thr,
    ss, sr, xos, xor_, yos, yor,
):
    a = lax.axis_index("tap")
    b = lax.axis_index("tm")
    y_hi = a // (NX * NZ)
    x = (a // NZ) % NX
    z = a % NZ
    y_lo = b // 2
    core = b % 2

    def tap_of(yh, xx, zz):
        return yh * (NX * NZ) + xx * NZ + zz

    b_next = (b + 1) % 8
    b_prev = (b + 7) % 8
    post = x % 2 == core
    far_tap = tap_of(1 - y_hi, x, z)
    z_up = tap_of(y_hi, x, (z + 1) % NZ)
    sibling = y_lo * 2 + (1 - core)

    fetch = pltpu.make_async_copy(p_ref, pbuf.at[x], ps.at[0])
    fetch.start()
    fetch_f = pltpu.make_async_copy(f_hbm, f_ref, ps.at[1])
    fetch_f.start()
    barrier = pltpu.get_barrier_semaphore()

    def hello(tap, tm):
        pl.semaphore_signal(barrier, inc=1, device_id=(tap, tm), device_id_type=MESH)

    for d in (1, 7, 2, 6, 3, 5, 4):
        hello(tap_of(y_hi, x, (z + d) % NZ), b)
    hello(far_tap, b)
    hello(a, b_next)
    hello(a, b_prev)
    for d in range(1, 4):
        hello(a, (b + 2 * d) % 8)
        hello(tap_of(y_hi, (x + d) % NX, z), b)

    fetch_f.wait()
    build_bands(f_ref, wbuf)
    fetch.wait()
    pl.semaphore_wait(barrier, 16)

    sends = []

    def go(copy):
        copy.start()
        sends.append(copy)

    def rows_of(c):
        return pl.ds(c * HALF, HALF)

    def hop(t, way, n):
        behind, dist, rows = HOPS[n]
        if rows is None:
            rows = 0 if way == 1 else 1
        span = pl.ds(0, ROWS) if rows == 2 else rows_of(rows)
        slot = (z + NZ - way * behind) % NZ
        dst = qbuf.at[t, slot, span]
        src = pbuf.at[x, span] if t == 0 and behind == 0 else dst
        i = (6 * t + n) * 2 + (way + 1) // 2
        return remote(
            src, dst, zs.at[i], zr.at[i], tap_of(y_hi, x, (z + NZ + way * dist) % NZ), b
        )

    def arrived(t, way, n):
        behind, dist, rows = HOPS[n]
        if rows is None:
            rows = 0 if way == 1 else 1
        span = pl.ds(0, ROWS) if rows == 2 else rows_of(rows)
        ref = qbuf.at[t, (z + NZ - way * (behind + dist)) % NZ, span]
        i = (6 * t + n) * 2 + (way + 1) // 2
        remote(ref, ref, zs.at[i], zr.at[i], z_up, b).wait_recv()

    def first_hops(t, *ns):
        for n in ns:
            for way in (1, -1):
                go(hop(t, way, n))

    def pass_on(t):
        for c in range(2):
            for way in (1, -1):
                arrived(t, way, c)
                if t == 0 and c == (1 - way) // 2:
                    go(hop(t, way, 5))
                go(hop(t, way, 3 + c))
        if t == 0:
            go(later_halo(6))
            go(later_halo(2))

    def wait_for(t, *ns):
        for n in ns:
            for way in (1, -1):
                arrived(t, way, n)

    def far(m, c):
        zz = (z + m) % NZ
        src = pbuf.at[x, rows_of(c)] if m == 0 else qbuf.at[0, zz, rows_of(c)]
        n = (2 if m else 0) + c
        return remote(src, qbuf.at[1, zz, rows_of(c)], cs.at[n], cr.at[n], far_tap, b)

    def from_far(m, c):
        ref = qbuf.at[1, (z + m) % NZ, rows_of(c)]
        n = (2 if m else 0) + c
        remote(ref, ref, cs.at[n], cr.at[n], far_tap, b).wait_recv()

    def owner_halo(m):
        d = NZ - m
        return remote(
            hq.at[1, z], hq.at[1, z], zhs.at[d - 1], zhr.at[d - 1],
            tap_of(y_hi, x, (z + d) % NZ), b,
        )

    def later_halo(m):
        zz = (z + m) % NZ
        return remote(
            qbuf.at[0, zz, :, pl.ds(0, HALO)], hq.at[0, zz], ths.at[m], thr.at[m], a, b_prev
        )

    def halo_from(t, m):
        if t == 1:
            ref = hq.at[1, (z + m) % NZ]
            remote(ref, ref, zhs.at[NZ - m - 1], zhr.at[NZ - m - 1], z_up, b).wait_recv()
        else:
            later_halo(m).wait_recv()

    def columns(t, *places):
        for m in places:
            if m:
                halo_from(t, m)
        val = details_of(
            jnp.concatenate([qbuf[t, (z + m) % NZ] for m in places], axis=0),
            jnp.concatenate([hq[t, (z + m) % NZ] for m in places], axis=0),
            wbuf,
        )
        for w in range(NWIN):
            for n, m in enumerate(places):
                first = (len(places) * w + n) * ROWS
                q, to = 2 * t + (m + 1) % NZ // 4, (m + 1) % 4 * ROWS
                for j in range(LEVELS):
                    dq[q, j, to : to + ROWS, w * OUT : (w + 1) * OUT] = (
                        val[first : first + ROWS, j * OUT : (j + 1) * OUT]
                    )

    def sib_copy(q):
        return remote(part.at[q], sib.at[q], ss.at[q], sr.at[q], a, sibling)

    def product(q):
        for j in range(LEVELS):
            part[q, j] = lax.dot_general(dp[j], dq[q, j], NT, preferred_element_type=jnp.float32)
        pl.when(jnp.logical_not(post))(lambda: sib_copy(q).start())

    def x_copy(q, d):
        there = (x + d) % NX
        return remote(
            red.at[q, there], xo.at[q, x // 2], xos.at[3 * q + d - 1], xor_.at[2 * q + x // 2],
            tap_of(y_hi, there, z), b,
        )

    def x_out(q):
        @pl.when(post)
        def _():
            sib_copy(q).wait_recv()
            for i in range(NX):
                rows = slice(i * ROWS, (i + 1) * ROWS)
                red[q, i] = part[q, :, rows] + sib[q, :, rows]
            for d in (2, 1, 3):
                x_copy(q, d).start()
            xo[q, x // 2] = red[q, x]

    def y_goal(q, i):
        return 2 * (y_hi if q < 2 else 1 - y_hi) + i

    def y_copy(q, i):
        goal = y_goal(q, i)
        d = (goal - y_lo + NYL) % NYL
        n = 3 * (q % 2) + d - 1
        return remote(
            xo.at[q, i], yo.at[q % 2, d - 1], yos.at[2 * q + i], yor.at[n], a, goal * 2 + core
        )

    def y_out(q):
        for i in range(2):
            @pl.when(2 * i + core != x)
            def _():
                ref = xo.at[q, i]
                remote(ref, ref, xos.at[0], xor_.at[2 * q + i], z_up, b).wait_recv()

            pl.when(y_goal(q, i) != y_lo)(lambda: y_copy(q, i).start())

    for c in range(2):
        go(far(0, c))
    go(remote(pbuf.at[x, :, pl.ds(0, HALO)], hp.at[x], hs.at[0], hr.at[0], a, b_prev))
    first_hops(0, 0, 1)
    for d in range(1, 4):
        go(remote(
            pbuf.at[x], pbuf.at[x], xs.at[d - 1], xr.at[d - 1], tap_of(y_hi, (x + d) % NX, z), b
        ))
    first_hops(0, 2)

    remote(hp.at[x], hp.at[x], hs.at[0], hr.at[0], a, b_prev).wait_recv()
    go(remote(hp.at[x], hq.at[1, z], chs.at[0], chr_.at[0], far_tap, b))
    for d in range(1, 4):
        go(remote(
            hp.at[x], hp.at[x], xhs.at[d - 1], xhr.at[d - 1], tap_of(y_hi, (x + d) % NX, z), b
        ))
    pass_on(0)
    for c in range(2):
        from_far(0, c)
        first_hops(1, c)
    first_hops(1, 2)
    wait_for(0, 2)
    go(later_halo(1))
    go(later_halo(7))
    for d in range(1, 4):
        ref = pbuf.at[(x + NX - d) % NX]
        remote(ref, ref, xs.at[d - 1], xr.at[d - 1], z_up, b).wait_recv()
    for d in range(1, 4):
        ref = hp.at[(x + NX - d) % NX]
        remote(ref, ref, xhs.at[d - 1], xhr.at[d - 1], z_up, b).wait_recv()
    val = details_of(
        jnp.concatenate([pbuf[i] for i in range(NX)], axis=0),
        jnp.concatenate([hp[i] for i in range(NX)], axis=0),
        wbuf,
    )
    for w in range(NWIN):
        for j in range(LEVELS):
            dp[j, :, w * OUT : (w + 1) * OUT] = val[
                w * NX * ROWS : (w + 1) * NX * ROWS, j * OUT : (j + 1) * OUT
            ]
    own = pl.ds(pl.multiple_of(x * ROWS, ROWS), ROWS)
    for j in range(LEVELS):
        dq[0, j, ROWS : 2 * ROWS] = dp[j, own, :]
    remote(hq.at[1, z], hq.at[1, z], chs.at[0], chr_.at[0], far_tap, b).wait_recv()
    for m in (2, 6, 1, 7, 3, 5, 4):
        go(owner_halo(m))
    columns(0, 2, 6)
    columns(0, 1, 7)
    product(0)
    for c in range(2):
        arrived(0, 1 - 2 * c, 5)
        go(far(4, c))
    go(later_halo(4))
    wait_for(0, 3, 4)
    go(later_halo(3))
    go(later_halo(5))
    pass_on(1)
    x_out(0)
    wait_for(1, 2)
    columns(1, 0, 2)
    columns(1, 1, 7)
    product(2)
    columns(1, 6)
    x_out(2)
    columns(0, 3, 5)
    columns(0, 4)
    product(1)
    y_out(0)
    wait_for(1, 3, 4)
    x_out(1)
    columns(1, 3, 5)
    for c in range(2):
        from_far(4, c)
    columns(1, 4)
    product(3)
    x_out(3)
    y_out(2)
    y_out(1)
    y_out(3)

    def sent(q):
        @pl.when(post)
        def _():
            for d in range(1, 4):
                x_copy(q, d).wait_send()

        pl.when(jnp.logical_not(post))(lambda: sib_copy(q).wait_send())

    def y_sent(q):
        for i in range(2):
            pl.when(y_goal(q, i) != y_lo)(lambda: y_copy(q, i).wait_send())

    for copy in sends:
        copy.wait_send()
    for q in range(CHUNKS):
        sent(q)
    for q in range(CHUNKS - 1):
        y_sent(q)

    kind = jnp.where(y_lo // 2 == y_hi, 0, 2)
    turn = ((z + NZ - 1) % NZ) * ROWS
    for h in range(2):
        for d in range(1, 4):
            ref = yo.at[h, d - 1]
            remote(ref, ref, yos.at[0], yor.at[3 * h + d - 1], a, sibling).wait_recv()
        if h == 0:
            first = xo[kind, y_lo % 2] + yo[0, 0] + yo[0, 1] + yo[0, 2]
    total = jnp.concatenate([first, xo[kind + 1, y_lo % 2] + yo[1, 0] + yo[1, 1] + yo[1, 2]], axis=2)
    total = total * (1.0 / (WIDTH * 8))
    for j in range(LEVELS):
        o_ref[j] = pltpu.roll(total[j], turn, 1)
    y_sent(CHUNKS - 1)


def body(pressure, filters):
    def sems(*counts):
        return [pltpu.SemaphoreType.DMA((n,)) for n in counts for _ in range(2)]

    f32, bf16 = jnp.float32, jnp.bfloat16
    return pl.pallas_call(
        kernel,
        out_shape=jax.ShapeDtypeStruct((LEVELS, ROWS, 256), f32),
        in_specs=[
            pl.BlockSpec(memory_space=pltpu.HBM),
            pl.BlockSpec(memory_space=pltpu.HBM),
        ],
        out_specs=pl.BlockSpec(memory_space=pltpu.VMEM),
        scratch_shapes=[
            pltpu.SMEM((2, FILT), f32),
            pltpu.VMEM((NX, ROWS, WIDTH), bf16),
            pltpu.VMEM((NX, ROWS, HALO), bf16),
            pltpu.VMEM((2, NZ, ROWS, WIDTH), bf16),
            pltpu.VMEM((2, NZ, ROWS, HALO), bf16),
            pltpu.VMEM((SPLITS, WIN, LEVELS * OUT), bf16),
            pltpu.VMEM((LEVELS, NX * ROWS, WIDTH), bf16),
            pltpu.VMEM((CHUNKS, LEVELS, 128, WIDTH), bf16),
            pltpu.VMEM((CHUNKS, LEVELS, NX * ROWS, 128), f32),
            pltpu.VMEM((CHUNKS, LEVELS, NX * ROWS, 128), f32),
            pltpu.VMEM((CHUNKS, NX, LEVELS, ROWS, 128), f32),
            pltpu.VMEM((CHUNKS, 2, LEVELS, ROWS, 128), f32),
            pltpu.VMEM((2, 3, LEVELS, ROWS, 128), f32),
            pltpu.SemaphoreType.DMA((2,)),
            *sems(1, 3, 3, 4, 1, 24, 7, 8, CHUNKS, 3 * CHUNKS, 2 * CHUNKS),
        ],
        compiler_params=pltpu.CompilerParams(
            collective_id=0, has_side_effects=True, vmem_limit_bytes=63 * 1024 * 1024
        ),
        cost_estimate=pl.CostEstimate(
            flops=4_000_000_000, bytes_accessed=200_000, transcendentals=0
        ),
    )(pressure, filters)


def solution(mesh):
    placed = (P("tap", "tm"), P())
    return jax.shard_map(
        body, mesh=mesh, in_specs=placed, out_specs=P(None, "tap", "tm"), check_vma=False
    )
```

```python
import jax
import jax.numpy as jnp
from jax import lax
from jax.experimental import pallas as pl
from jax.experimental.pallas import tpu as pltpu
from jax.sharding import PartitionSpec as P

FILT = 16
LEVELS = 3
NX, NZ, NYL = 4, 8, 4
ROWS = 32
WIDTH = 1024
HALO = 128
WIN = 256
OUT = 128
NWIN = WIDTH // OUT
SPLITS = 2
LANES = 384
CHUNKS = 4
HALF = 16
HOPS = ((0, 2, 0), (0, 2, 1), (0, 1, 2), (2, 1, 0), (2, 1, 1), (2, 2, None))
MESH = pl.DeviceIdType.MESH
NT = (((1,), (1,)), ((), ()))


def remote(src, dst, send, recv, tap, tm):
    return pltpu.make_async_remote_copy(
        src_ref=src, dst_ref=dst, send_sem=send, recv_sem=recv,
        device_id=(tap, tm), device_id_type=MESH,
    )


def build_bands(f_ref, wbuf):
    lane = lax.broadcasted_iota(jnp.int32, (8, LANES), 1)

    def comb(row, top, step):
        line = jnp.zeros((8, LANES), jnp.float32)
        for k in range(FILT):
            line = jnp.where(lane == top - step * k, f_ref[row, k], line)
        return line

    def smoothed(line, step):
        total = jnp.zeros((8, LANES), jnp.float32)
        for k in range(FILT):
            moved = line if k == 0 else pltpu.roll(line, LANES - step * k, 1)
            total = total + f_ref[1, k] * moved
        return total

    lines = [
        comb(0, 328, 1),
        smoothed(comb(0, 344, 2), 1),
        smoothed(smoothed(comb(0, 376, 4), 2), 1),
    ]
    for level, line in enumerate(lines):
        wide = jnp.broadcast_to(line[0:1, :], (WIN, LANES))
        band = pltpu.roll(wide, 0, 1, stride=1, stride_axis=0)[:, :OUT]
        for piece in range(SPLITS):
            part = band.astype(jnp.bfloat16)
            wbuf[piece, :, level * OUT : (level + 1) * OUT] = part
            band = band - part.astype(jnp.float32)


def details_of(main, halo, wbuf):
    ext = jnp.concatenate([main, halo], axis=1)
    windows = jnp.concatenate([ext[:, w * OUT : w * OUT + WIN] for w in range(NWIN)], axis=0)
    total = jnp.dot(windows, wbuf[0], preferred_element_type=jnp.float32)
    for piece in range(1, SPLITS):
        total += jnp.dot(windows, wbuf[piece], preferred_element_type=jnp.float32)
    return total.astype(jnp.bfloat16)


def kernel(
    p_ref, f_hbm, o_ref,
    f_ref, pbuf, hp, qbuf, hq, wbuf, dp, dq, part, sib, red, xo, yo,
    ps, hs, hr, xs, xr, xhs, xhr, cs, cr, chs, chr_, zs, zr, zhs, zhr, ths, thr,
    ss, sr, xos, xor_, yos, yor,
):
    a = lax.axis_index("tap")
    b = lax.axis_index("tm")
    y_hi = a // (NX * NZ)
    x = (a // NZ) % NX
    z = a % NZ
    y_lo = b // 2
    core = b % 2

    def tap_of(yh, xx, zz):
        return yh * (NX * NZ) + xx * NZ + zz

    b_next = (b + 1) % 8
    b_prev = (b + 7) % 8
    post = x % 2 == core
    far_tap = tap_of(1 - y_hi, x, z)
    z_up = tap_of(y_hi, x, (z + 1) % NZ)
    sibling = y_lo * 2 + (1 - core)

    fetch = pltpu.make_async_copy(p_ref, pbuf.at[x], ps.at[0])
    fetch.start()
    fetch_f = pltpu.make_async_copy(f_hbm, f_ref, ps.at[1])
    fetch_f.start()
    barrier = pltpu.get_barrier_semaphore()

    def hello(tap, tm):
        pl.semaphore_signal(barrier, inc=1, device_id=(tap, tm), device_id_type=MESH)

    for d in (1, 7, 2, 6, 3, 5, 4):
        hello(tap_of(y_hi, x, (z + d) % NZ), b)
    hello(far_tap, b)
    hello(a, b_next)
    hello(a, b_prev)
    for d in range(1, 4):
        hello(a, (b + 2 * d) % 8)
        hello(tap_of(y_hi, (x + d) % NX, z), b)

    fetch_f.wait()
    build_bands(f_ref, wbuf)
    fetch.wait()
    pl.semaphore_wait(barrier, 16)

    sends = []

    def go(copy):
        copy.start()
        sends.append(copy)

    def rows_of(c):
        return pl.ds(c * HALF, HALF)

    def hop(t, way, n):
        behind, dist, rows = HOPS[n]
        if rows is None:
            rows = 0 if way == 1 else 1
        span = pl.ds(0, ROWS) if rows == 2 else rows_of(rows)
        slot = (z + NZ - way * behind) % NZ
        dst = qbuf.at[t, slot, span]
        src = pbuf.at[x, span] if t == 0 and behind == 0 else dst
        i = (6 * t + n) * 2 + (way + 1) // 2
        return remote(
            src, dst, zs.at[i], zr.at[i], tap_of(y_hi, x, (z + NZ + way * dist) % NZ), b
        )

    def arrived(t, way, n):
        behind, dist, rows = HOPS[n]
        if rows is None:
            rows = 0 if way == 1 else 1
        span = pl.ds(0, ROWS) if rows == 2 else rows_of(rows)
        ref = qbuf.at[t, (z + NZ - way * (behind + dist)) % NZ, span]
        i = (6 * t + n) * 2 + (way + 1) // 2
        remote(ref, ref, zs.at[i], zr.at[i], z_up, b).wait_recv()

    def first_hops(t, *ns):
        for n in ns:
            for way in (1, -1):
                go(hop(t, way, n))

    def pass_on(t):
        for c in range(2):
            for way in (1, -1):
                arrived(t, way, c)
                if t == 0 and c == (1 - way) // 2:
                    go(hop(t, way, 5))
                go(hop(t, way, 3 + c))
        if t == 0:
            go(later_halo(6))
            go(later_halo(2))

    def wait_for(t, *ns):
        for n in ns:
            for way in (1, -1):
                arrived(t, way, n)

    def far(m, c):
        zz = (z + m) % NZ
        src = pbuf.at[x, rows_of(c)] if m == 0 else qbuf.at[0, zz, rows_of(c)]
        n = (2 if m else 0) + c
        return remote(src, qbuf.at[1, zz, rows_of(c)], cs.at[n], cr.at[n], far_tap, b)

    def from_far(m, c):
        ref = qbuf.at[1, (z + m) % NZ, rows_of(c)]
        n = (2 if m else 0) + c
        remote(ref, ref, cs.at[n], cr.at[n], far_tap, b).wait_recv()

    def owner_halo(m):
        d = NZ - m
        return remote(
            hq.at[1, z], hq.at[1, z], zhs.at[d - 1], zhr.at[d - 1],
            tap_of(y_hi, x, (z + d) % NZ), b,
        )

    def later_halo(m):
        zz = (z + m) % NZ
        return remote(
            qbuf.at[0, zz, :, pl.ds(0, HALO)], hq.at[0, zz], ths.at[m], thr.at[m], a, b_prev
        )

    def halo_from(t, m):
        if t == 1:
            ref = hq.at[1, (z + m) % NZ]
            remote(ref, ref, zhs.at[NZ - m - 1], zhr.at[NZ - m - 1], z_up, b).wait_recv()
        else:
            later_halo(m).wait_recv()

    def columns(t, *places):
        for m in places:
            if m:
                halo_from(t, m)
        val = details_of(
            jnp.concatenate([qbuf[t, (z + m) % NZ] for m in places], axis=0),
            jnp.concatenate([hq[t, (z + m) % NZ] for m in places], axis=0),
            wbuf,
        )
        for w in range(NWIN):
            for n, m in enumerate(places):
                first = (len(places) * w + n) * ROWS
                q, to = 2 * t + (m + 1) % NZ // 4, (m + 1) % 4 * ROWS
                for j in range(LEVELS):
                    dq[q, j, to : to + ROWS, w * OUT : (w + 1) * OUT] = (
                        val[first : first + ROWS, j * OUT : (j + 1) * OUT]
                    )

    def parts(q):
        return range(LEVELS) if q == CHUNKS - 1 else (None,)

    def pick(ref, j):
        return ref if j is None else ref.at[j]

    def sib_copy(q, j):
        n = q + (j or 0)
        return remote(
            pick(part.at[q], j), pick(sib.at[q], j), ss.at[n], sr.at[n], a, sibling
        )

    def product(q):
        for j in range(LEVELS):
            part[q, j] = lax.dot_general(dp[j], dq[q, j], NT, preferred_element_type=jnp.float32)
            if j in parts(q):
                pl.when(jnp.logical_not(post))(lambda: sib_copy(q, j).start())
        if None in parts(q):
            pl.when(jnp.logical_not(post))(lambda: sib_copy(q, None).start())

    def x_copy(q, j, d):
        there = (x + d) % NX
        n = q + (j or 0)
        return remote(
            pick(red.at[q, there], j), pick(xo.at[q, x // 2], j),
            xos.at[3 * n + d - 1], xor_.at[2 * n + x // 2], tap_of(y_hi, there, z), b,
        )

    def x_out(q):
        @pl.when(post)
        def _():
            for j in parts(q):
                sib_copy(q, j).wait_recv()
                for i in range(NX):
                    rows = slice(i * ROWS, (i + 1) * ROWS)
                    for level in range(LEVELS) if j is None else (j,):
                        red[q, i, level] = part[q, level, rows] + sib[q, level, rows]
                for d in (2, 1, 3):
                    x_copy(q, j, d).start()
            xo[q, x // 2] = red[q, x]

    def y_goal(q, i):
        return 2 * (y_hi if q < 2 else 1 - y_hi) + i

    def y_copy(q, i):
        goal = y_goal(q, i)
        d = (goal - y_lo + NYL) % NYL
        n = 3 * (q % 2) + d - 1
        return remote(
            xo.at[q, i], yo.at[q % 2, d - 1], yos.at[2 * q + i], yor.at[n], a, goal * 2 + core
        )

    def y_out(q):
        for i in range(2):
            @pl.when(2 * i + core != x)
            def _():
                for j in parts(q):
                    ref = pick(xo.at[q, i], j)
                    n = q + (j or 0)
                    remote(ref, ref, xos.at[0], xor_.at[2 * n + i], z_up, b).wait_recv()

            pl.when(y_goal(q, i) != y_lo)(lambda: y_copy(q, i).start())

    for c in range(2):
        go(far(0, c))
    go(remote(pbuf.at[x, :, pl.ds(0, HALO)], hp.at[x], hs.at[0], hr.at[0], a, b_prev))
    first_hops(0, 0, 1)
    for d in range(1, 4):
        go(remote(
            pbuf.at[x], pbuf.at[x], xs.at[d - 1], xr.at[d - 1], tap_of(y_hi, (x + d) % NX, z), b
        ))
    first_hops(0, 2)

    remote(hp.at[x], hp.at[x], hs.at[0], hr.at[0], a, b_prev).wait_recv()
    go(remote(hp.at[x], hq.at[1, z], chs.at[0], chr_.at[0], far_tap, b))
    for d in range(1, 4):
        go(remote(
            hp.at[x], hp.at[x], xhs.at[d - 1], xhr.at[d - 1], tap_of(y_hi, (x + d) % NX, z), b
        ))
    pass_on(0)
    for c in range(2):
        from_far(0, c)
        first_hops(1, c)
    first_hops(1, 2)
    wait_for(0, 2)
    go(later_halo(1))
    go(later_halo(7))
    for d in range(1, 4):
        ref = pbuf.at[(x + NX - d) % NX]
        remote(ref, ref, xs.at[d - 1], xr.at[d - 1], z_up, b).wait_recv()
    for d in range(1, 4):
        ref = hp.at[(x + NX - d) % NX]
        remote(ref, ref, xhs.at[d - 1], xhr.at[d - 1], z_up, b).wait_recv()
    val = details_of(
        jnp.concatenate([pbuf[i] for i in range(NX)], axis=0),
        jnp.concatenate([hp[i] for i in range(NX)], axis=0),
        wbuf,
    )
    for w in range(NWIN):
        for j in range(LEVELS):
            dp[j, :, w * OUT : (w + 1) * OUT] = val[
                w * NX * ROWS : (w + 1) * NX * ROWS, j * OUT : (j + 1) * OUT
            ]
    own = pl.ds(pl.multiple_of(x * ROWS, ROWS), ROWS)
    for j in range(LEVELS):
        dq[0, j, ROWS : 2 * ROWS] = dp[j, own, :]
    remote(hq.at[1, z], hq.at[1, z], chs.at[0], chr_.at[0], far_tap, b).wait_recv()
    for m in (2, 6, 1, 7, 3, 5, 4):
        go(owner_halo(m))
    columns(0, 2, 6)
    columns(0, 1, 7)
    product(0)
    for c in range(2):
        arrived(0, 1 - 2 * c, 5)
        go(far(4, c))
    go(later_halo(4))
    wait_for(0, 3, 4)
    go(later_halo(3))
    go(later_halo(5))
    pass_on(1)
    x_out(0)
    wait_for(1, 2)
    columns(1, 0, 2)
    columns(1, 1, 7)
    product(2)
    columns(1, 6)
    x_out(2)
    columns(0, 3, 5)
    columns(0, 4)
    product(1)
    y_out(0)
    wait_for(1, 3, 4)
    x_out(1)
    columns(1, 3, 5)
    for c in range(2):
        from_far(4, c)
    columns(1, 4)
    product(3)
    x_out(3)
    y_out(2)
    y_out(1)
    y_out(3)

    def sent(q):
        @pl.when(post)
        def _():
            for j in parts(q):
                for d in range(1, 4):
                    x_copy(q, j, d).wait_send()

        for j in parts(q):
            pl.when(jnp.logical_not(post))(lambda: sib_copy(q, j).wait_send())

    def y_sent(q):
        for i in range(2):
            pl.when(y_goal(q, i) != y_lo)(lambda: y_copy(q, i).wait_send())

    for copy in sends:
        copy.wait_send()
    for q in range(CHUNKS):
        sent(q)
    for q in range(CHUNKS - 1):
        y_sent(q)

    kind = jnp.where(y_lo // 2 == y_hi, 0, 2)
    turn = ((z + NZ - 1) % NZ) * ROWS
    for h in range(2):
        for d in range(1, 4):
            ref = yo.at[h, d - 1]
            remote(ref, ref, yos.at[0], yor.at[3 * h + d - 1], a, sibling).wait_recv()
        if h == 0:
            first = xo[kind, y_lo % 2] + yo[0, 0] + yo[0, 1] + yo[0, 2]
    total = jnp.concatenate([first, xo[kind + 1, y_lo % 2] + yo[1, 0] + yo[1, 1] + yo[1, 2]], axis=2)
    total = total * (1.0 / (WIDTH * 8))
    for j in range(LEVELS):
        o_ref[j] = pltpu.roll(total[j], turn, 1)
    y_sent(CHUNKS - 1)


def body(pressure, filters):
    def sems(*counts):
        return [pltpu.SemaphoreType.DMA((n,)) for n in counts for _ in range(2)]

    f32, bf16 = jnp.float32, jnp.bfloat16
    return pl.pallas_call(
        kernel,
        out_shape=jax.ShapeDtypeStruct((LEVELS, ROWS, 256), f32),
        in_specs=[
            pl.BlockSpec(memory_space=pltpu.HBM),
            pl.BlockSpec(memory_space=pltpu.HBM),
        ],
        out_specs=pl.BlockSpec(memory_space=pltpu.VMEM),
        scratch_shapes=[
            pltpu.SMEM((2, FILT), f32),
            pltpu.VMEM((NX, ROWS, WIDTH), bf16),
            pltpu.VMEM((NX, ROWS, HALO), bf16),
            pltpu.VMEM((2, NZ, ROWS, WIDTH), bf16),
            pltpu.VMEM((2, NZ, ROWS, HALO), bf16),
            pltpu.VMEM((SPLITS, WIN, LEVELS * OUT), bf16),
            pltpu.VMEM((LEVELS, NX * ROWS, WIDTH), bf16),
            pltpu.VMEM((CHUNKS, LEVELS, 128, WIDTH), bf16),
            pltpu.VMEM((CHUNKS, LEVELS, NX * ROWS, 128), f32),
            pltpu.VMEM((CHUNKS, LEVELS, NX * ROWS, 128), f32),
            pltpu.VMEM((CHUNKS, NX, LEVELS, ROWS, 128), f32),
            pltpu.VMEM((CHUNKS, 2, LEVELS, ROWS, 128), f32),
            pltpu.VMEM((2, 3, LEVELS, ROWS, 128), f32),
            pltpu.SemaphoreType.DMA((2,)),
            *sems(1, 3, 3, 4, 1, 24, 7, 8, CHUNKS + 2, 3 * CHUNKS + 6, 2 * CHUNKS + 4),
        ],
        compiler_params=pltpu.CompilerParams(
            collective_id=0, has_side_effects=True, vmem_limit_bytes=63 * 1024 * 1024
        ),
        cost_estimate=pl.CostEstimate(
            flops=4_000_000_000, bytes_accessed=200_000, transcendentals=0
        ),
    )(pressure, filters)


def solution(mesh):
    placed = (P("tap", "tm"), P())
    return jax.shard_map(
        body, mesh=mesh, in_specs=placed, out_specs=P(None, "tap", "tm"), check_vma=False
    )
```
